32 devices in a mesh: grp: 2 (over y), ka: 4 (over z), aux: 2 (over x), orb: 2 (over core).
Axes of the slice: x: 2, y: 2, z: 4, core: 2. Of those that a mesh axis runs over, the one named last changes fastest.
Arguments:
- chol_tiles: bfloat16 [4, 4, 1536, 384], P('grp', 'ka', 'aux', 'orb'), parts along dimension 0, may hold values from -6 to 6
- tile_exps: int32 [4, 4, 12], P('grp', 'ka', 'aux'), parts along dimension 0, may hold values from -2 to 2
- amplitudes: bfloat16 [4, 4, 4, 96, 96], P('grp', 'ka'), parts along dimension 0, may hold values from -0.3125 to 0.3125
- pair_table: int32 [4, 4], replicated, may hold values from 0 to 3, as said below
Outputs:
- dressed: bfloat16 [4, 4, 1536, 384], P('grp', 'ka', 'aux', 'orb'), parts along dimension 0
- cycle_block: float32 [4, 4, 96, 96], P('grp', 'ka', ('aux', 'orb')), parts along dimension 0
The draws below stay inside these ranges and needn't reach their ends.
There are 2 independent parts, one for each index of `grp`. The reference program is written for one: setup_inputs(seed, part) draws one part's arguments, and reference() takes and returns one part's arrays. A program takes and returns all parts, laid end to end along the dimension named above; an argument that names none is the same for every part. Nothing has to cross between parts.
Inputs may be any that keep to these rules, and one draw needn't show every extreme that they name: pair_table[k, k2] is the label of the k-point whose momentum is that of k minus that of k2 on a closed lattice of 4 points; each row and column is a permutation.
All inputs are finite; a program needn't handle non-finite values.
Results may differ from the reference program's by a relative error of at most 0.008.
Values may be sent and summed in bfloat16 or wider, within the bound.
A program may use at most 64 MiB of HBM per device.

```python
import jax
import jax.numpy as jnp

OCC = 96
VIR = 384
NQT = 2
NK = 4
QTOT = 16


def draw_pair_table(key, part):
    key = jax.random.fold_in(key, 5)
    labels = jax.random.permutation(key, NK).astype(jnp.int32)
    inverse = jnp.argsort(labels, stable=True).astype(jnp.int32)
    differ = (labels[:, None] - labels[None, :]) % NK
    return inverse[differ].astype(jnp.int32)


def touch_ends(result, stream_key, least, top_value):
    shape = result.shape
    place = [jax.random.randint(jax.random.fold_in(stream_key, axis), (), 0, shape[axis]) for axis in range(len(shape))]
    result = result.at[tuple(place)].set(least)
    longest = shape.index(max(shape))
    place[longest] = (place[longest] + 1) % shape[longest]
    return result.at[tuple(place)].set(top_value)


def shard_levels(stream_key, shape, pieces, low, top_value):
    def one(dim, parts):
        steps = jax.random.uniform(jax.random.fold_in(jax.random.fold_in(stream_key, 6), dim), (parts,), jnp.float32, low / len(pieces), top_value / len(pieces))
        return jnp.repeat(jnp.exp(steps), shape[dim] // parts).reshape((-1,) + (1,) * (len(shape) - dim - 1))

    gain = one(*pieces[0])
    for cut in pieces[1:]:
        gain = gain * one(*cut)
    return gain


def noise(own_key, shape, spread, bound, shards=(), dtype=jnp.bfloat16):
    result = jax.random.normal(own_key, shape, jnp.float32) * spread
    if len(shards) > 0:
        result = shard_levels(own_key, shape, shards, -0.22, 0.18) * result
    return jnp.clip(result, min=-bound, max=bound).astype(dtype)


def setup_inputs(seed: int = 0, part: int = 0) -> dict:
    keys = jax.random.split(jax.random.key(seed), 5)
    part_keys = jax.random.split(jax.random.fold_in(keys[4], part), 5)
    chol_tiles = noise(part_keys[0], (NQT, NK, QTOT * OCC, VIR), 1.0, 6.0, ((1, 4), (2, 2), (3, 2)))
    tile_exps = touch_ends(jax.random.randint(part_keys[1], (NQT, NK, QTOT * OCC // 128), -2, 3), jax.random.fold_in(part_keys[1], 1), -2, 2).astype(jnp.int32)
    amplitudes = noise(part_keys[2], (NQT, NK, NK, OCC, OCC), (NK * OCC) ** -0.5, 0.3125, ((1, 4),))
    pair_table = draw_pair_table(jax.random.fold_in(keys[4], 71), part)
    return dict(chol_tiles=chol_tiles, tile_exps=tile_exps, amplitudes=amplitudes, pair_table=pair_table)


def reference(chol_tiles, tile_exps, amplitudes, pair_table):
    scale = jnp.repeat(jnp.exp2(tile_exps.astype(jnp.float32)), 128, axis=-1)[..., None]
    chol = (chol_tiles.astype(jnp.float32) * scale).astype(jnp.bfloat16)
    nq, nk, rows, vir = chol_tiles.shape
    occ = amplitudes.shape[-1]
    qtot = rows // occ
    blocks = chol.astype(jnp.float32).reshape(nq, nk, qtot, occ, vir)
    kidx = jnp.arange(nk).astype(jnp.int32)[:, None]
    chosen = amplitudes[:, kidx, pair_table].astype(jnp.float32)
    dressed = jnp.einsum('nkmij,nmqja->nkqia', chosen, blocks).astype(jnp.bfloat16)
    cycle = jnp.einsum('nkqia,nkqja->nkij', dressed.astype(jnp.float32), blocks)
    cycle = cycle * (1.0 / jnp.sqrt(jnp.float32(qtot * vir)))
    return (dressed.reshape(nq, nk, rows, vir), cycle)
```

```python
import functools

import jax
import jax.numpy as jnp
from jax import lax
from jax.experimental import pallas as pl
from jax.experimental.pallas import tpu as pltpu
from jax.sharding import PartitionSpec as P

MESH = pl.DeviceIdType.MESH
GROUP = 128
LANES = 128


def passed_along(shard, axis, by):
    devices = lax.axis_size(axis)
    return lax.ppermute(shard, axis, [(i, (i + by) % devices) for i in range(devices)])


def rescale(tile, exps):
    scale = jnp.repeat(jnp.exp2(exps.astype(jnp.float32)), GROUP, axis=-1)[..., None]
    return (tile.astype(jnp.float32) * scale).astype(jnp.bfloat16)


def ring_body(chol_tiles, tile_exps, amplitudes, pair_table):
    nk = lax.axis_size("ka")
    mine = lax.axis_index("ka")
    nq, _, rows, vdev = chol_tiles.shape
    occ = amplitudes.shape[-1]
    qdev = rows // occ
    row_table = lax.dynamic_index_in_dim(pair_table, mine, 0, keepdims=False)
    own = rescale(chol_tiles, tile_exps)
    amp_rows = amplitudes[:, 0]

    def contribute(total, scaled, source):
        slot = row_table[source]
        amp = lax.dynamic_index_in_dim(amp_rows, slot, 1, keepdims=False)
        blocks = scaled[:, 0].reshape(nq, qdev, occ, vdev)
        return total + jnp.einsum("nij,nqja->nqia", amp, blocks, preferred_element_type=jnp.float32)

    def advance(step, carry):
        parcel, total = carry
        total = contribute(total, rescale(*parcel), (mine - step) % nk)
        parcel = passed_along(parcel, "ka", 1)
        return (parcel, total)

    empty = jnp.zeros((nq, qdev, occ, vdev), jnp.float32)
    parcel, total = lax.fori_loop(0, nk - 1, advance, ((chol_tiles, tile_exps), empty))
    total = contribute(total, rescale(*parcel), (mine - (nk - 1)) % nk)
    dressed = total.astype(jnp.bfloat16)
    blocks = own[:, 0].reshape(nq, qdev, occ, vdev)
    norm = 1.0 / jnp.sqrt(jnp.float32(qdev * lax.axis_size("aux") * vdev * lax.axis_size("orb")))
    partial_cycle = (
        jnp.einsum("nqia,nqja->nij", dressed, blocks, preferred_element_type=jnp.float32) * norm
    )
    cycle = lax.psum_scatter(
        partial_cycle[:, None].astype(jnp.bfloat16), ("aux", "orb"), scatter_dimension=2, tiled=True
    ).astype(jnp.float32)
    return (dressed.reshape(nq, 1, rows, vdev), cycle)


def line_kernel(
    dims, chol, amps, scale, table, dressed, cycle,
    tiles, own, rin, parts, asel, ain, wide, stage, pre, cyc, csend, crecv,
    load_sem, store_sem, own_sem, fwd_sem, part_sem, in_sem, amp_sems, csend_sem, crecv_sem,
):
    nq, occ, vdev, pairs, norm = dims
    pieces = nq * pairs
    rem = vdev - LANES
    step = 32
    half = occ // step
    me = lax.axis_index("ka")
    aux = lax.axis_index("aux")
    orb = lax.axis_index("orb")
    is_end = jnp.logical_or(me == 0, me == 3)
    is_mid = jnp.logical_not(is_end)
    near = 1 + me // 3
    outer = 3 * (me // 2)
    across = 3 - me
    peers = [(1 - aux, orb), (aux, 1 - orb), (1 - aux, 1 - orb)]

    def load(p):
        rows = pl.ds(pl.multiple_of((p % pairs) * 2 * occ, 2 * occ), 2 * occ)
        return pltpu.make_async_copy(chol.at[p // pairs, 0, rows, :], tiles.at[p], load_sem.at[p])

    def store(p):
        rows = pl.ds(pl.multiple_of((p % pairs) * 2 * occ, 2 * occ), 2 * occ)
        return pltpu.make_async_copy(stage.at[p], dressed.at[p // pairs, 0, rows, :], store_sem.at[p])

    def send(src, slot, p, sem, to):
        return pltpu.make_async_remote_copy(
            src_ref=src.at[p], dst_ref=rin.at[slot, p], send_sem=sem.at[p], recv_sem=in_sem.at[slot, p],
            device_id={"ka": to}, device_id_type=MESH,
        )

    def amp_send(to):
        return pltpu.make_async_remote_copy(
            src_ref=asel, dst_ref=ain, send_sem=amp_sems.at[0], recv_sem=amp_sems.at[1],
            device_id={"ka": to}, device_id_type=MESH,
        )

    def loop(n, fn):
        lax.fori_loop(0, n, lambda p, c: (fn(p), c)[1], 0)

    loop(pieces, lambda p: load(p).start())

    barrier = pltpu.get_barrier_semaphore()
    for a, o in peers:
        pl.semaphore_signal(barrier, inc=1, device_id={"aux": a, "orb": o}, device_id_type=MESH)

    @pl.when(is_end)
    def _():
        pl.semaphore_signal(barrier, inc=1, device_id={"ka": near}, device_id_type=MESH)

    @pl.when(is_mid)
    def _():
        pl.semaphore_signal(barrier, inc=1, device_id={"ka": outer}, device_id_type=MESH)
        pl.semaphore_signal(barrier, inc=1, device_id={"ka": across}, device_id_type=MESH)

    def amp(q, source):
        return amps[q, 0, table[me, source]]

    @pl.when(is_end)
    def _():
        for q in range(nq):
            for slot, source in enumerate((near, 3 - near, 3 - me)):
                asel[slot, q] = amp(q, source)

    @pl.when(is_mid)
    def _():
        for q in range(nq):
            for slot, source in enumerate((me, across, 3 - outer)):
                wide[slot, q, pl.ds(0, occ), :] = amp(q, source)

    def pack(p):
        load(p).wait()
        q, t = p // pairs, p % pairs
        for i in range(half):
            def rows(n):
                s = scale[q, 0, (2 * half * t + n) * step // GROUP]
                return tiles[p, pl.ds(n * step, step), :].astype(jnp.float32) * s
            even, odd = rows(i), rows(i + half)
            here = pl.ds(i * step, step)
            own[p, here, pl.ds(0, LANES)] = even[:, :LANES].astype(jnp.bfloat16)
            own[p, here, pl.ds(LANES, LANES)] = odd[:, :LANES].astype(jnp.bfloat16)
            tail = jnp.concatenate([even[:, LANES:], odd[:, LANES:]], axis=1)
            own[p, here, pl.ds(2 * LANES, 2 * rem)] = tail.astype(jnp.bfloat16)

    def dot(a, b):
        return jnp.dot(a, b, preferred_element_type=jnp.float32)

    cyc[...] = jnp.zeros_like(cyc)

    def finish(p, total):
        q = p // pairs
        y = total.astype(jnp.bfloat16)
        cyc[q] += lax.dot_general(y, own[p], (((1,), (1,)), ((), ())), preferred_element_type=jnp.float32)
        stage[p, pl.ds(0, occ), pl.ds(0, LANES)] = y[:, :LANES]
        stage[p, pl.ds(occ, occ), pl.ds(0, LANES)] = y[:, LANES:2 * LANES]
        stage[p, pl.ds(0, occ), pl.ds(LANES, rem)] = total[:, 2 * LANES:2 * LANES + rem].astype(jnp.bfloat16)
        stage[p, pl.ds(occ, occ), pl.ds(LANES, rem)] = total[:, 2 * LANES + rem:].astype(jnp.bfloat16)
        store(p).start()

    pl.semaphore_wait(barrier, 4 + jnp.where(is_mid, 1, 0))

    @pl.when(is_end)
    def _():
        amp_send(near).start()

        def out(p):
            pack(p)
            send(own, 0, p, own_sem, near).start()

        loop(pieces, out)

        def first(p):
            pre[p] = dot(amp(p // pairs, me), own[p])

        loop(pieces, first)

        def last(p):
            send(own, 0, p, own_sem, near).wait_recv()
            finish(p, pre[p] + rin[0, p].astype(jnp.float32))

        loop(pieces, last)

    @pl.when(is_mid)
    def _():
        def out(p):
            pack(p)
            send(own, 1, p, own_sem, across).start()

        loop(pieces, out)
        amp_send(outer).wait_recv()
        for q in range(nq):
            for slot in range(3):
                wide[slot, q, pl.ds(occ, occ), :] = ain[slot, q]

        def forward(p):
            send(own, 0, p, own_sem, outer).wait_recv()
            send(rin.at[0], 2, p, fwd_sem, across).start()

        loop(pieces, forward)

        def last(p):
            q = p // pairs
            both = dot(wide[0, q], own[p])
            mine = dot(amp(q, outer), rin[0, p])
            send(own, 1, p, own_sem, across).wait_recv()
            both += dot(wide[1, q], rin[1, p])
            send(own, 2, p, own_sem, across).wait_recv()
            both += dot(wide[2, q], rin[2, p])
            parts[p] = both[occ:].astype(jnp.bfloat16)
            send(parts, 0, p, part_sem, outer).start()
            finish(p, both[:occ] + mine)

        loop(pieces, last)

    part = occ // 4

    def quarter(a, o):
        rows = pl.ds(pl.multiple_of((2 * a + o) * part, 8), part)
        return jnp.concatenate([cyc[q, rows, :] for q in range(nq)], axis=0)

    def trade(n):
        a, o = peers[n]
        return pltpu.make_async_remote_copy(
            src_ref=csend.at[n], dst_ref=crecv.at[n], send_sem=csend_sem.at[n], recv_sem=crecv_sem.at[n],
            device_id={"aux": a, "orb": o}, device_id_type=MESH,
        )

    for n, (a, o) in enumerate(peers):
        csend[n] = quarter(a, o).astype(jnp.bfloat16)
        trade(n).start()
    total = quarter(aux, orb)
    for n in range(3):
        trade(n).wait_recv()
        total += crecv[n].astype(jnp.float32)
    for q in range(nq):
        cycle[q, 0] = total[q * part:(q + 1) * part] * norm

    for n in range(3):
        trade(n).wait_send()
    loop(pieces, lambda p: store(p).wait())
    loop(pieces, lambda p: send(own, 0, p, own_sem, near).wait_send())

    @pl.when(is_end)
    def _():
        amp_send(near).wait_send()

    @pl.when(is_mid)
    def _():
        loop(pieces, lambda p: send(own, 2, p, fwd_sem, across).wait_send())
        loop(pieces, lambda p: send(own, 0, p, part_sem, outer).wait_send())


def line_body(chol_tiles, tile_exps, amplitudes, pair_table):
    nq, _, rows, vdev = chol_tiles.shape
    occ = amplitudes.shape[-1]
    pairs = rows // occ // 2
    pieces = nq * pairs
    width = 2 * vdev
    devices = lax.axis_size("aux") * lax.axis_size("orb")
    norm = (rows // occ * vdev * devices) ** -0.5
    scale = jnp.exp2(tile_exps.astype(jnp.float32))
    bf16, f32 = jnp.bfloat16, jnp.float32
    dma = pltpu.SemaphoreType.DMA
    part = occ // devices
    return pl.pallas_call(
        functools.partial(line_kernel, (nq, occ, vdev, pairs, norm)),
        out_shape=(
            jax.ShapeDtypeStruct(chol_tiles.shape, bf16),
            jax.ShapeDtypeStruct((nq, 1, part, occ), f32),
        ),
        in_specs=[
            pl.BlockSpec(memory_space=pl.ANY),
            pl.BlockSpec(memory_space=pltpu.VMEM),
            pl.BlockSpec(memory_space=pltpu.SMEM),
            pl.BlockSpec(memory_space=pltpu.SMEM),
        ],
        out_specs=(pl.BlockSpec(memory_space=pl.ANY), pl.BlockSpec(memory_space=pltpu.VMEM)),
        scratch_shapes=[
            pltpu.VMEM((pieces, 2 * occ, vdev), bf16),
            pltpu.VMEM((pieces, occ, width), bf16),
            pltpu.VMEM((3, pieces, occ, width), bf16),
            pltpu.VMEM((pieces, occ, width), bf16),
            pltpu.VMEM((3, nq, occ, occ), bf16),
            pltpu.VMEM((3, nq, occ, occ), bf16),
            pltpu.VMEM((3, nq, 2 * occ, occ), bf16),
            pltpu.VMEM((pieces, 2 * occ, vdev), bf16),
            pltpu.VMEM((pieces, occ, width), f32),
            pltpu.VMEM((nq, occ, occ), f32),
            pltpu.VMEM((3, nq * part, occ), bf16),
            pltpu.VMEM((3, nq * part, occ), bf16),
            dma((pieces,)),
            dma((pieces,)),
            dma((pieces,)),
            dma((pieces,)),
            dma((pieces,)),
            dma((3, pieces)),
            dma((2,)),
            dma((3,)),
            dma((3,)),
        ],
        compiler_params=pltpu.CompilerParams(
            collective_id=0, has_side_effects=True, vmem_limit_bytes=24 * 1024 * 1024
        ),
        cost_estimate=pl.CostEstimate(
            flops=2 * 8 * occ * occ * width * pieces, bytes_accessed=4 * rows * nq * vdev, transcendentals=0
        ),
    )(chol_tiles, amplitudes, scale, pair_table)


def solution(mesh):
    def body(chol_tiles, tile_exps, amplitudes, pair_table):
        nq, _, rows, vdev = chol_tiles.shape
        occ = amplitudes.shape[-1]
        line = mesh.shape["ka"] == 4 and mesh.shape["aux"] == 2 and mesh.shape["orb"] == 2
        fits = rows % (2 * occ) == 0 and vdev == LANES + LANES // 2 and occ % 32 == 0
        chosen = line_body if line and fits else ring_body
        return chosen(chol_tiles, tile_exps, amplitudes, pair_table)

    return jax.shard_map(
        body,
        mesh=mesh,
        in_specs=(
            P("grp", "ka", "aux", "orb"),
            P("grp", "ka", "aux"),
            P("grp", "ka", None, None, None),
            P(),
        ),
        out_specs=(P("grp", "ka", "aux", "orb"), P("grp", "ka", ("aux", "orb"), None)),
        check_vma=False,
    )
```

```python
import functools
import math

import jax
import jax.numpy as jnp
from jax import lax
from jax.experimental import pallas as pl
from jax.experimental.pallas import tpu as pltpu
from jax.sharding import PartitionSpec as P

MESH = pl.DeviceIdType.MESH
GROUP = 128
LANES = 128
ROWS_EACH = 96
LAG = 2


def passed_along(shard, axis, by):
    devices = lax.axis_size(axis)
    return lax.ppermute(shard, axis, [(i, (i + by) % devices) for i in range(devices)])


def rescale(tile, exps):
    scale = jnp.repeat(jnp.exp2(exps.astype(jnp.float32)), GROUP, axis=-1)[..., None]
    return (tile.astype(jnp.float32) * scale).astype(jnp.bfloat16)


def ring_body(chol_tiles, tile_exps, amplitudes, pair_table):
    nk = lax.axis_size("ka")
    mine = lax.axis_index("ka")
    nq, _, rows, vdev = chol_tiles.shape
    occ = amplitudes.shape[-1]
    qdev = rows // occ
    row_table = lax.dynamic_index_in_dim(pair_table, mine, 0, keepdims=False)
    own = rescale(chol_tiles, tile_exps)
    amp_rows = amplitudes[:, 0]

    def contribute(total, scaled, source):
        slot = row_table[source]
        amp = lax.dynamic_index_in_dim(amp_rows, slot, 1, keepdims=False)
        blocks = scaled[:, 0].reshape(nq, qdev, occ, vdev)
        return total + jnp.einsum("nij,nqja->nqia", amp, blocks, preferred_element_type=jnp.float32)

    def advance(step, carry):
        parcel, total = carry
        total = contribute(total, rescale(*parcel), (mine - step) % nk)
        parcel = passed_along(parcel, "ka", 1)
        return (parcel, total)

    empty = jnp.zeros((nq, qdev, occ, vdev), jnp.float32)
    parcel, total = lax.fori_loop(0, nk - 1, advance, ((chol_tiles, tile_exps), empty))
    total = contribute(total, rescale(*parcel), (mine - (nk - 1)) % nk)
    dressed = total.astype(jnp.bfloat16)
    blocks = own[:, 0].reshape(nq, qdev, occ, vdev)
    norm = 1.0 / jnp.sqrt(jnp.float32(qdev * lax.axis_size("aux") * vdev * lax.axis_size("orb")))
    partial_cycle = (
        jnp.einsum("nqia,nqja->nij", dressed, blocks, preferred_element_type=jnp.float32) * norm
    )
    cycle = lax.psum_scatter(
        partial_cycle[:, None].astype(jnp.bfloat16), ("aux", "orb"), scatter_dimension=2, tiled=True
    ).astype(jnp.float32)
    return (dressed.reshape(nq, 1, rows, vdev), cycle)


def line_kernel(
    dims, chol, amps, exps, table, dressed, cycle,
    tiles, own, rin, parts, asel, ain, wide, mine, stage, pre, acc, cyc, csend, crecv,
    load_sem, store_sem, own_sem, fwd_sem, part_sem, in_sem, amp_sems, csend_sem, crecv_sem,
):
    nq, occ, vdev, width, groups, rows_each, norm = dims
    splits = vdev // rows_each
    pieces = nq * groups * splits
    blocks = width // occ
    me = lax.axis_index("ka")
    aux = lax.axis_index("aux")
    orb = lax.axis_index("orb")
    is_end = jnp.logical_or(me == 0, me == 3)
    is_mid = jnp.logical_not(is_end)
    near = 1 + me // 3
    outer = 3 * (me // 2)
    across = 3 - me
    peers = [(1 - aux, orb), (aux, 1 - orb), (1 - aux, 1 - orb)]

    def q_of(p):
        return p // (groups * splits)

    def group_of(p):
        return p // splits % groups

    def window(ref, p):
        high = pl.ds(pl.multiple_of(p % splits * rows_each, rows_each), rows_each)
        lanes = pl.ds(pl.multiple_of(group_of(p) * width, width), width)
        return ref.at[q_of(p), 0, high, lanes]

    def load(p):
        return pltpu.make_async_copy(window(chol, p), tiles.at[p], load_sem.at[p])

    def store(p):
        return pltpu.make_async_copy(stage.at[p], window(dressed, p), store_sem.at[p])

    def send(src, slot, p, sem, to):
        return pltpu.make_async_remote_copy(
            src_ref=src.at[p], dst_ref=rin.at[slot, p], send_sem=sem.at[p], recv_sem=in_sem.at[slot, p],
            device_id={"ka": to}, device_id_type=MESH,
        )

    def amp_send(to):
        return pltpu.make_async_remote_copy(
            src_ref=asel, dst_ref=ain, send_sem=amp_sems.at[0], recv_sem=amp_sems.at[1],
            device_id={"ka": to}, device_id_type=MESH,
        )

    def loop(n, fn):
        lax.fori_loop(0, n, lambda p, c: (fn(p), c)[1], 0)

    loop(pieces, lambda p: load(p).start())

    barrier = pltpu.get_barrier_semaphore()
    for a, o in peers:
        pl.semaphore_signal(barrier, inc=1, device_id={"aux": a, "orb": o}, device_id_type=MESH)

    @pl.when(is_end)
    def _():
        pl.semaphore_signal(barrier, inc=1, device_id={"ka": near}, device_id_type=MESH)

    @pl.when(is_mid)
    def _():
        pl.semaphore_signal(barrier, inc=1, device_id={"ka": outer}, device_id_type=MESH)
        pl.semaphore_signal(barrier, inc=1, device_id={"ka": across}, device_id_type=MESH)

    def amp(q, source):
        return amps[q, 0, table[me, source]]

    @pl.when(is_end)
    def _():
        for q in range(nq):
            for slot, source in enumerate((near, 3 - near, 3 - me)):
                asel[slot, q] = amp(q, source)

    def pack(p):
        load(p).wait()
        for n in range(width // LANES):
            here = pl.ds(n * LANES, LANES)
            shift = exps[q_of(p), 0, group_of(p) * (width // LANES) + n] + 8
            s = lax.shift_left(1, shift).astype(jnp.float32) * (1.0 / 256.0)
            own[p, :, here] = (tiles[p, :, here].astype(jnp.float32) * s).astype(jnp.bfloat16)

    def spread(ref, at, block):
        block = block.astype(jnp.float32)
        for n in range(blocks):
            strips = []
            if n > 0:
                strips.append(jnp.zeros((occ, n * occ), jnp.float32))
            strips.append(block)
            if n < blocks - 1:
                strips.append(jnp.zeros((occ, (blocks - 1 - n) * occ), jnp.float32))
            ref[(*at, pl.ds(n * occ, occ), slice(None))] = jnp.concatenate(strips, axis=1).astype(jnp.bfloat16)

    def dot(x, w):
        return lax.dot_general(x, w, (((1,), (1,)), ((), ())), preferred_element_type=jnp.float32)

    def finish(p, total):
        y = total.astype(jnp.bfloat16)
        stage[p] = y
        store(p).start()
        acc[q_of(p)] += lax.dot_general(y, own[p], (((0,), (0,)), ((), ())), preferred_element_type=jnp.float32)

    pl.semaphore_wait(barrier, 4 + jnp.where(is_mid, 1, 0))

    @pl.when(is_end)
    def _():
        def out(p):
            pack(p)
            send(own, 0, p, own_sem, near).start()

        out(0)
        amp_send(near).start()
        loop(pieces - 1, lambda p: out(p + 1))
        acc[...] = jnp.zeros_like(acc)
        for q in range(nq):
            spread(mine, (q,), amp(q, me))

        def first(p):
            pre[p] = dot(own[p], mine[q_of(p)])

        loop(pieces, first)

        def last(p):
            send(own, 0, p, own_sem, near).wait_recv()
            finish(p, pre[p] + rin[0, p].astype(jnp.float32))

        loop(pieces, last)

    @pl.when(is_mid)
    def _():
        def out(p):
            send(own, 1, p, own_sem, across).start()

        pack(0)
        out(0)
        pack(1)
        out(1)
        loop(pieces - 2, lambda p: pack(p + 2))
        acc[...] = jnp.zeros_like(acc)
        for q in range(nq):
            spread(mine, (q,), amp(q, outer))
            for slot, source in enumerate((me, across, 3 - outer)):
                spread(wide, (slot, q, 0), amp(q, source))
        amp_send(outer).wait_recv()
        for q in range(nq):
            for slot in range(3):
                spread(wide, (slot, q, 1), ain[slot, q])

        def forward(p):
            send(own, 0, p, own_sem, outer).wait_recv()
            send(rin.at[0], 2, p, fwd_sem, across).start()

            @pl.when(p + 2 < pieces)
            def _():
                out(p + 2)

        def last(p):
            q = q_of(p)
            here = dot(own[p], wide[0, q, 0]) + dot(rin[0, p], mine[q])
            there = dot(own[p], wide[0, q, 1])
            send(own, 1, p, own_sem, across).wait_recv()
            there += dot(rin[1, p], wide[1, q, 1])
            here += dot(rin[1, p], wide[1, q, 0])
            send(own, 2, p, own_sem, across).wait_recv()
            parts[p] = (there + dot(rin[2, p], wide[2, q, 1])).astype(jnp.bfloat16)
            send(parts, 0, p, part_sem, outer).start()
            finish(p, here + dot(rin[2, p], wide[2, q, 0]))

        def turn(p):
            @pl.when(p < pieces)
            def _():
                forward(p)

            @pl.when(p >= LAG)
            def _():
                last(p - LAG)

        loop(pieces + LAG, turn)

    part = occ // 4
    for q in range(nq):
        cyc[q] = sum(acc[q, n * occ:(n + 1) * occ, n * occ:(n + 1) * occ] for n in range(blocks))

    def quarter(a, o):
        rows = pl.ds(pl.multiple_of((2 * a + o) * part, 8), part)
        return jnp.concatenate([cyc[q, rows, :] for q in range(nq)], axis=0)

    def trade(n):
        a, o = peers[n]
        return pltpu.make_async_remote_copy(
            src_ref=csend.at[n], dst_ref=crecv.at[n], send_sem=csend_sem.at[n], recv_sem=crecv_sem.at[n],
            device_id={"aux": a, "orb": o}, device_id_type=MESH,
        )

    for n, (a, o) in enumerate(peers):
        csend[n] = quarter(a, o).astype(jnp.bfloat16)
        trade(n).start()
    total = quarter(aux, orb)
    for n in range(3):
        trade(n).wait_recv()
        total += crecv[n].astype(jnp.float32)
    for q in range(nq):
        cycle[q, 0] = total[q * part:(q + 1) * part] * norm

    for n in range(3):
        trade(n).wait_send()
    loop(pieces, lambda p: store(p).wait())
    loop(pieces, lambda p: send(own, 0, p, own_sem, near).wait_send())

    @pl.when(is_end)
    def _():
        amp_send(near).wait_send()

    @pl.when(is_mid)
    def _():
        loop(pieces, lambda p: send(own, 2, p, fwd_sem, across).wait_send())
        loop(pieces, lambda p: send(own, 0, p, part_sem, outer).wait_send())


def line_body(chol_tiles, tile_exps, amplitudes, pair_table):
    nq, _, rows, vdev = chol_tiles.shape
    occ = amplitudes.shape[-1]
    width = math.lcm(occ, LANES)
    groups = rows // width
    pieces = nq * groups * (vdev // ROWS_EACH)
    devices = lax.axis_size("aux") * lax.axis_size("orb")
    norm = (rows // occ * vdev * devices) ** -0.5
    bf16, f32 = jnp.bfloat16, jnp.float32
    dma = pltpu.SemaphoreType.DMA
    part = occ // devices
    turned = jnp.swapaxes(chol_tiles, 2, 3)
    dressed, cycle = pl.pallas_call(
        functools.partial(line_kernel, (nq, occ, vdev, width, groups, ROWS_EACH, norm)),
        out_shape=(
            jax.ShapeDtypeStruct(turned.shape, bf16),
            jax.ShapeDtypeStruct((nq, 1, part, occ), f32),
        ),
        in_specs=[
            pl.BlockSpec(memory_space=pltpu.HBM),
            pl.BlockSpec(memory_space=pltpu.VMEM),
            pl.BlockSpec(memory_space=pltpu.SMEM),
            pl.BlockSpec(memory_space=pltpu.SMEM),
        ],
        out_specs=(pl.BlockSpec(memory_space=pltpu.HBM), pl.BlockSpec(memory_space=pltpu.VMEM)),
        scratch_shapes=[
            pltpu.VMEM((pieces, ROWS_EACH, width), bf16),
            pltpu.VMEM((pieces, ROWS_EACH, width), bf16),
            pltpu.VMEM((3, pieces, ROWS_EACH, width), bf16),
            pltpu.VMEM((pieces, ROWS_EACH, width), bf16),
            pltpu.VMEM((3, nq, occ, occ), bf16),
            pltpu.VMEM((3, nq, occ, occ), bf16),
            pltpu.VMEM((3, nq, 2, width, width), bf16),
            pltpu.VMEM((nq, width, width), bf16),
            pltpu.VMEM((pieces, ROWS_EACH, width), bf16),
            pltpu.VMEM((pieces, ROWS_EACH, width), f32),
            pltpu.VMEM((nq, width, width), f32),
            pltpu.VMEM((nq, occ, occ), f32),
            pltpu.VMEM((3, nq * part, occ), bf16),
            pltpu.VMEM((3, nq * part, occ), bf16),
            dma((pieces,)),
            dma((pieces,)),
            dma((pieces,)),
            dma((pieces,)),
            dma((pieces,)),
            dma((3, pieces)),
            dma((2,)),
            dma((3,)),
            dma((3,)),
        ],
        compiler_params=pltpu.CompilerParams(
            collective_id=0, has_side_effects=True, vmem_limit_bytes=24 * 1024 * 1024
        ),
        cost_estimate=pl.CostEstimate(
            flops=2 * 8 * occ * rows * vdev * nq, bytes_accessed=4 * rows * nq * vdev, transcendentals=0
        ),
    )(turned, amplitudes, tile_exps, pair_table)
    return jnp.swapaxes(dressed, 2, 3), cycle


def solution(mesh):
    def body(chol_tiles, tile_exps, amplitudes, pair_table):
        nq, _, rows, vdev = chol_tiles.shape
        occ = amplitudes.shape[-1]
        line = mesh.shape["ka"] == 4 and mesh.shape["aux"] == 2 and mesh.shape["orb"] == 2
        fits = rows % math.lcm(occ, LANES) == 0 and vdev % ROWS_EACH == 0 and occ % 32 == 0
        chosen = line_body if line and fits else ring_body
        return chosen(chol_tiles, tile_exps, amplitudes, pair_table)

    return jax.shard_map(
        body,
        mesh=mesh,
        in_specs=(
            P("grp", "ka", "aux", "orb"),
            P("grp", "ka", "aux"),
            P("grp", "ka", None, None, None),
            P(),
        ),
        out_specs=(P("grp", "ka", "aux", "orb"), P("grp", "ka", ("aux", "orb"), None)),
        check_vma=False,
    )
```

```python
import functools
import math

import jax
import jax.numpy as jnp
from jax import lax
from jax.experimental import pallas as pl
from jax.experimental.pallas import tpu as pltpu
from jax.sharding import PartitionSpec as P

MESH = pl.DeviceIdType.MESH
GROUP = 128
LANES = 128
ROWS_EACH = 96
BUNCH = 1


def passed_along(shard, axis, by):
    devices = lax.axis_size(axis)
    return lax.ppermute(shard, axis, [(i, (i + by) % devices) for i in range(devices)])


def rescale(tile, exps):
    scale = jnp.repeat(jnp.exp2(exps.astype(jnp.float32)), GROUP, axis=-1)[..., None]
    return (tile.astype(jnp.float32) * scale).astype(jnp.bfloat16)


def ring_body(chol_tiles, tile_exps, amplitudes, pair_table):
    nk = lax.axis_size("ka")
    mine = lax.axis_index("ka")
    nq, _, rows, vdev = chol_tiles.shape
    occ = amplitudes.shape[-1]
    qdev = rows // occ
    row_table = lax.dynamic_index_in_dim(pair_table, mine, 0, keepdims=False)
    own = rescale(chol_tiles, tile_exps)
    amp_rows = amplitudes[:, 0]

    def contribute(total, scaled, source):
        slot = row_table[source]
        amp = lax.dynamic_index_in_dim(amp_rows, slot, 1, keepdims=False)
        blocks = scaled[:, 0].reshape(nq, qdev, occ, vdev)
        return total + jnp.einsum("nij,nqja->nqia", amp, blocks, preferred_element_type=jnp.float32)

    def advance(step, carry):
        parcel, total = carry
        total = contribute(total, rescale(*parcel), (mine - step) % nk)
        parcel = passed_along(parcel, "ka", 1)
        return (parcel, total)

    empty = jnp.zeros((nq, qdev, occ, vdev), jnp.float32)
    parcel, total = lax.fori_loop(0, nk - 1, advance, ((chol_tiles, tile_exps), empty))
    total = contribute(total, rescale(*parcel), (mine - (nk - 1)) % nk)
    dressed = total.astype(jnp.bfloat16)
    blocks = own[:, 0].reshape(nq, qdev, occ, vdev)
    norm = 1.0 / jnp.sqrt(jnp.float32(qdev * lax.axis_size("aux") * vdev * lax.axis_size("orb")))
    partial_cycle = (
        jnp.einsum("nqia,nqja->nij", dressed, blocks, preferred_element_type=jnp.float32) * norm
    )
    cycle = lax.psum_scatter(
        partial_cycle[:, None].astype(jnp.bfloat16), ("aux", "orb"), scatter_dimension=2, tiled=True
    ).astype(jnp.float32)
    return (dressed.reshape(nq, 1, rows, vdev), cycle)


def line_kernel(
    dims, chol, amps_far, exps_far, table_far, dressed, cycle,
    exps, table, tiles, amps, own, rin, parts, asel, ain, wide, mine, stage, pre, pre_there, acc, cyc, csend, crecv,
    load_sem, store_sem, own_sem, fwd_sem, part_sem, in_sem, amp_sems, csend_sem, crecv_sem, amp_load_sem,
):
    nq, occ, vdev, width, groups, rows_each, norm = dims
    splits = vdev // rows_each
    pieces = nq * groups * splits
    blocks = width // occ
    me = lax.axis_index("ka")
    aux = lax.axis_index("aux")
    orb = lax.axis_index("orb")
    is_end = jnp.logical_or(me == 0, me == 3)
    is_mid = jnp.logical_not(is_end)
    near = 1 + me // 3
    outer = 3 * (me // 2)
    across = 3 - me
    peers = [(1 - aux, orb), (aux, 1 - orb), (1 - aux, 1 - orb)]

    def q_of(p):
        return p // (groups * splits)

    def group_of(p):
        return p // splits % groups

    def window(ref, p):
        high = pl.ds(pl.multiple_of(p % splits * rows_each, rows_each), rows_each)
        lanes = pl.ds(pl.multiple_of(group_of(p) * width, width), width)
        return ref.at[q_of(p), 0, high, lanes]

    def load(p):
        return pltpu.make_async_copy(window(chol, p), tiles.at[p], load_sem.at[p])

    def store(p):
        return pltpu.make_async_copy(stage.at[p], window(dressed, p), store_sem.at[p])

    def send(src, slot, p, sem, to):
        return pltpu.make_async_remote_copy(
            src_ref=src.at[p], dst_ref=rin.at[slot, p], send_sem=sem.at[p], recv_sem=in_sem.at[slot, p],
            device_id={"ka": to}, device_id_type=MESH,
        )

    def amp_send(to):
        return pltpu.make_async_remote_copy(
            src_ref=asel, dst_ref=ain, send_sem=amp_sems.at[0], recv_sem=amp_sems.at[1],
            device_id={"ka": to}, device_id_type=MESH,
        )

    def loop(n, fn):
        lax.fori_loop(0, n, lambda p, c: (fn(p), c)[1], 0)

    barrier = pltpu.get_barrier_semaphore()
    for a, o in peers:
        pl.semaphore_signal(barrier, inc=1, device_id={"aux": a, "orb": o}, device_id_type=MESH)

    @pl.when(is_end)
    def _():
        pl.semaphore_signal(barrier, inc=1, device_id={"ka": near}, device_id_type=MESH)

    @pl.when(is_mid)
    def _():
        pl.semaphore_signal(barrier, inc=1, device_id={"ka": outer}, device_id_type=MESH)
        pl.semaphore_signal(barrier, inc=1, device_id={"ka": across}, device_id_type=MESH)

    small = [
        pltpu.make_async_copy(far, here, amp_load_sem.at[n])
        for n, (far, here) in enumerate(((exps_far, exps), (table_far, table), (amps_far, amps)))
    ]
    for copy in small:
        copy.start()
    loop(pieces, lambda p: load(p).start())

    def amp(q, source):
        return amps[q, 0, table[me, source]]

    for copy in small:
        copy.wait()

    @pl.when(is_end)
    def _():
        for q in range(nq):
            for slot, source in enumerate((near, 3 - near, 3 - me)):
                asel[slot, q] = amp(q, source)

    def pack(p):
        load(p).wait()
        for n in range(width // LANES):
            here = pl.ds(n * LANES, LANES)
            shift = exps[q_of(p), 0, group_of(p) * (width // LANES) + n] + 8
            s = lax.shift_left(1, shift).astype(jnp.float32) * (1.0 / 256.0)
            own[p, :, here] = (tiles[p, :, here].astype(jnp.float32) * s).astype(jnp.bfloat16)

    def spread(ref, at, block):
        block = block.astype(jnp.float32)
        for n in range(blocks):
            strips = []
            if n > 0:
                strips.append(jnp.zeros((occ, n * occ), jnp.float32))
            strips.append(block)
            if n < blocks - 1:
                strips.append(jnp.zeros((occ, (blocks - 1 - n) * occ), jnp.float32))
            ref[(*at, pl.ds(n * occ, occ), slice(None))] = jnp.concatenate(strips, axis=1).astype(jnp.bfloat16)

    def dot(x, w):
        return lax.dot_general(x, w, (((1,), (1,)), ((), ())), preferred_element_type=jnp.float32)

    def bunch(ref, m):
        return ref[pl.ds(m * BUNCH, BUNCH)].reshape(BUNCH * rows_each, width)

    def put(ref, m, value):
        ref[pl.ds(m * BUNCH, BUNCH)] = value.reshape(BUNCH, rows_each, width)

    def finish(p, total):
        y = total.astype(jnp.bfloat16)
        stage[p] = y
        store(p).start()
        acc[q_of(p)] += lax.dot_general(y, own[p], (((0,), (0,)), ((), ())), preferred_element_type=jnp.float32)

    part = occ // 4

    def quarter(q, a, o):
        return cyc[q, pl.ds(pl.multiple_of((2 * a + o) * part, 8), part), :]

    def trade(q, n):
        a, o = peers[n]
        return pltpu.make_async_remote_copy(
            src_ref=csend.at[q, n], dst_ref=crecv.at[q, n], send_sem=csend_sem.at[q, n], recv_sem=crecv_sem.at[q, n],
            device_id={"aux": a, "orb": o}, device_id_type=MESH,
        )

    def share(q):
        cyc[q] = sum(acc[q, n * occ:(n + 1) * occ, n * occ:(n + 1) * occ] for n in range(blocks))
        for n, (a, o) in enumerate(peers):
            csend[q, n] = quarter(q, a, o)
            trade(q, n).start()

    def by_system(fn):
        each = pieces // nq
        for q in range(nq):
            lax.fori_loop(q * each, (q + 1) * each, lambda p, c: (fn(p), c)[1], 0)
            share(q)

    pl.semaphore_wait(barrier, 4 + jnp.where(is_mid, 1, 0))

    @pl.when(is_end)
    def _():
        def out(p):
            pack(p)
            send(own, 0, p, own_sem, near).start()

        out(0)
        amp_send(near).start()
        loop(pieces - 1, lambda p: out(p + 1))
        acc[...] = jnp.zeros_like(acc)
        for q in range(nq):
            spread(mine, (q,), amp(q, me))

        loop(pieces // BUNCH, lambda m: put(pre, m, dot(bunch(own, m), mine[q_of(m * BUNCH)])))

        def last(p):
            send(own, 0, p, own_sem, near).wait_recv()
            finish(p, pre[p] + rin[0, p].astype(jnp.float32))

        by_system(last)

    @pl.when(is_mid)
    def _():
        def out(p):
            send(own, 1, p, own_sem, across).start()

        loop(pieces, lambda p: (pack(p), out(p)))
        acc[...] = jnp.zeros_like(acc)
        for q in range(nq):
            spread(mine, (q,), amp(q, outer))
            for slot, source in enumerate((me, across, 3 - outer)):
                spread(wide, (slot, q, 0), amp(q, source))
        amp_send(outer).wait_recv()
        for q in range(nq):
            for slot in range(3):
                spread(wide, (slot, q, 1), ain[slot, q])

        def early(m):
            for n in range(BUNCH):
                p = m * BUNCH + n
                send(own, 0, p, own_sem, outer).wait_recv()
                send(rin.at[0], 2, p, fwd_sem, across).start()
            q = q_of(m * BUNCH)
            x = bunch(own, m)
            there = dot(x, wide[0, q, 1])
            here = dot(x, wide[0, q, 0]) + dot(bunch(rin.at[0], m), mine[q])
            for n in range(BUNCH):
                send(own, 1, m * BUNCH + n, own_sem, across).wait_recv()
            x = bunch(rin.at[1], m)
            put(pre_there, m, there + dot(x, wide[1, q, 1]))
            put(pre, m, here + dot(x, wide[1, q, 0]))

        loop(pieces // BUNCH, early)

        def last(p):
            q = q_of(p)
            send(own, 2, p, own_sem, across).wait_recv()
            parts[p] = (pre_there[p] + dot(rin[2, p], wide[2, q, 1])).astype(jnp.bfloat16)
            send(parts, 0, p, part_sem, outer).start()
            finish(p, pre[p] + dot(rin[2, p], wide[2, q, 0]))

        by_system(last)

    for q in range(nq):
        total = quarter(q, aux, orb)
        for n in range(3):
            trade(q, n).wait_recv()
            total += crecv[q, n]
        cycle[q, 0] = total * norm

    for q in range(nq):
        for n in range(3):
            trade(q, n).wait_send()
    loop(pieces, lambda p: store(p).wait())
    loop(pieces, lambda p: send(own, 0, p, own_sem, near).wait_send())

    @pl.when(is_end)
    def _():
        amp_send(near).wait_send()

    @pl.when(is_mid)
    def _():
        loop(pieces, lambda p: send(own, 2, p, fwd_sem, across).wait_send())
        loop(pieces, lambda p: send(own, 0, p, part_sem, outer).wait_send())


def line_body(chol_tiles, tile_exps, amplitudes, pair_table):
    nq, _, rows, vdev = chol_tiles.shape
    occ = amplitudes.shape[-1]
    width = math.lcm(occ, LANES)
    groups = rows // width
    pieces = nq * groups * (vdev // ROWS_EACH)
    devices = lax.axis_size("aux") * lax.axis_size("orb")
    norm = (rows // occ * vdev * devices) ** -0.5
    bf16, f32 = jnp.bfloat16, jnp.float32
    dma = pltpu.SemaphoreType.DMA
    part = occ // devices
    turned = jnp.swapaxes(chol_tiles, 2, 3)
    dressed, cycle = pl.pallas_call(
        functools.partial(line_kernel, (nq, occ, vdev, width, groups, ROWS_EACH, norm)),
        out_shape=(
            jax.ShapeDtypeStruct(turned.shape, bf16),
            jax.ShapeDtypeStruct((nq, 1, part, occ), f32),
        ),
        in_specs=[
            pl.BlockSpec(memory_space=pltpu.HBM),
            pl.BlockSpec(memory_space=pltpu.HBM),
            pl.BlockSpec(memory_space=pltpu.HBM),
            pl.BlockSpec(memory_space=pltpu.HBM),
        ],
        out_specs=(pl.BlockSpec(memory_space=pltpu.HBM), pl.BlockSpec(memory_space=pltpu.VMEM)),
        scratch_shapes=[
            pltpu.SMEM(tile_exps.shape, jnp.int32),
            pltpu.SMEM(pair_table.shape, jnp.int32),
            pltpu.VMEM((pieces, ROWS_EACH, width), bf16),
            pltpu.VMEM(amplitudes.shape, bf16),
            pltpu.VMEM((pieces, ROWS_EACH, width), bf16),
            pltpu.VMEM((3, pieces, ROWS_EACH, width), bf16),
            pltpu.VMEM((pieces, ROWS_EACH, width), bf16),
            pltpu.VMEM((3, nq, occ, occ), bf16),
            pltpu.VMEM((3, nq, occ, occ), bf16),
            pltpu.VMEM((3, nq, 2, width, width), bf16),
            pltpu.VMEM((nq, width, width), bf16),
            pltpu.VMEM((pieces, ROWS_EACH, width), bf16),
            pltpu.VMEM((pieces, ROWS_EACH, width), f32),
            pltpu.VMEM((pieces, ROWS_EACH, width), f32),
            pltpu.VMEM((nq, width, width), f32),
            pltpu.VMEM((nq, occ, occ), f32),
            pltpu.VMEM((nq, 3, part, occ), f32),
            pltpu.VMEM((nq, 3, part, occ), f32),
            dma((pieces,)),
            dma((pieces,)),
            dma((pieces,)),
            dma((pieces,)),
            dma((pieces,)),
            dma((3, pieces)),
            dma((2,)),
            dma((nq, 3)),
            dma((nq, 3)),
            dma((3,)),
        ],
        compiler_params=pltpu.CompilerParams(
            collective_id=0, has_side_effects=True, vmem_limit_bytes=60 * 1024 * 1024
        ),
        cost_estimate=pl.CostEstimate(
            flops=2 * 8 * occ * rows * vdev * nq, bytes_accessed=4 * rows * nq * vdev, transcendentals=0
        ),
    )(turned, amplitudes, tile_exps, pair_table)

    def hand_on(near_out, near_cycle, far_out, far_cycle, held, held_cycle, sems):
        parts = [(q, 0, pl.ds(n * vdev // 2, vdev // 2)) for q in range(nq) for n in range(2)]
        trips = [(near_cycle, held_cycle, far_cycle)] + [(near_out.at[i], held.at[i], far_out.at[i]) for i in parts]
        ins = [pltpu.make_async_copy(a, b, sems.at[0, n]) for n, (a, b, _) in enumerate(trips)]
        outs = [pltpu.make_async_copy(b, c, sems.at[1, n]) for n, (_, b, c) in enumerate(trips)]
        for copy in ins:
            copy.start()
        for before, after in zip(ins, outs):
            before.wait()
            after.start()
        for copy in outs:
            copy.wait()

    dressed, cycle = pl.pallas_call(
        hand_on,
        out_shape=(
            jax.ShapeDtypeStruct(dressed.shape, dressed.dtype),
            jax.ShapeDtypeStruct(cycle.shape, cycle.dtype),
        ),
        in_specs=[pl.BlockSpec(memory_space=pltpu.HBM)] * 2,
        out_specs=(pl.BlockSpec(memory_space=pltpu.HBM),) * 2,
        scratch_shapes=[
            pltpu.VMEM(dressed.shape, dressed.dtype),
            pltpu.VMEM(cycle.shape, cycle.dtype),
            dma((2, 1 + 2 * nq)),
        ],
        compiler_params=pltpu.CompilerParams(vmem_limit_bytes=60 * 1024 * 1024),
        name="hand_on",
    )(dressed, cycle)
    return jnp.swapaxes(dressed, 2, 3), cycle


def solution(mesh):
    def body(chol_tiles, tile_exps, amplitudes, pair_table):
        nq, _, rows, vdev = chol_tiles.shape
        occ = amplitudes.shape[-1]
        line = mesh.shape["ka"] == 4 and mesh.shape["aux"] == 2 and mesh.shape["orb"] == 2
        fits = rows % math.lcm(occ, LANES) == 0 and vdev % (BUNCH * ROWS_EACH) == 0 and occ % 32 == 0
        chosen = line_body if line and fits else ring_body
        return chosen(chol_tiles, tile_exps, amplitudes, pair_table)

    return jax.shard_map(
        body,
        mesh=mesh,
        in_specs=(
            P("grp", "ka", "aux", "orb"),
            P("grp", "ka", "aux"),
            P("grp", "ka", None, None, None),
            P(),
        ),
        out_specs=(P("grp", "ka", "aux", "orb"), P("grp", "ka", ("aux", "orb"), None)),
        check_vma=False,
    )
```

```python
import functools
import math

import jax
import jax.numpy as jnp
from jax import lax
from jax.experimental import pallas as pl
from jax.experimental.pallas import tpu as pltpu
from jax.sharding import PartitionSpec as P

MESH = pl.DeviceIdType.MESH
GROUP = 128
LANES = 128
ROWS_EACH = 96
AHEAD = 5
LAG = 4
BUNCH = 1


def passed_along(shard, axis, by):
    devices = lax.axis_size(axis)
    return lax.ppermute(shard, axis, [(i, (i + by) % devices) for i in range(devices)])


def rescale(tile, exps):
    scale = jnp.repeat(jnp.exp2(exps.astype(jnp.float32)), GROUP, axis=-1)[..., None]
    return (tile.astype(jnp.float32) * scale).astype(jnp.bfloat16)


def ring_body(chol_tiles, tile_exps, amplitudes, pair_table):
    nk = lax.axis_size("ka")
    mine = lax.axis_index("ka")
    nq, _, rows, vdev = chol_tiles.shape
    occ = amplitudes.shape[-1]
    qdev = rows // occ
    row_table = lax.dynamic_index_in_dim(pair_table, mine, 0, keepdims=False)
    own = rescale(chol_tiles, tile_exps)
    amp_rows = amplitudes[:, 0]

    def contribute(total, scaled, source):
        slot = row_table[source]
        amp = lax.dynamic_index_in_dim(amp_rows, slot, 1, keepdims=False)
        blocks = scaled[:, 0].reshape(nq, qdev, occ, vdev)
        return total + jnp.einsum("nij,nqja->nqia", amp, blocks, preferred_element_type=jnp.float32)

    def advance(step, carry):
        parcel, total = carry
        total = contribute(total, rescale(*parcel), (mine - step) % nk)
        parcel = passed_along(parcel, "ka", 1)
        return (parcel, total)

    empty = jnp.zeros((nq, qdev, occ, vdev), jnp.float32)
    parcel, total = lax.fori_loop(0, nk - 1, advance, ((chol_tiles, tile_exps), empty))
    total = contribute(total, rescale(*parcel), (mine - (nk - 1)) % nk)
    dressed = total.astype(jnp.bfloat16)
    blocks = own[:, 0].reshape(nq, qdev, occ, vdev)
    norm = 1.0 / jnp.sqrt(jnp.float32(qdev * lax.axis_size("aux") * vdev * lax.axis_size("orb")))
    partial_cycle = (
        jnp.einsum("nqia,nqja->nij", dressed, blocks, preferred_element_type=jnp.float32) * norm
    )
    cycle = lax.psum_scatter(
        partial_cycle[:, None].astype(jnp.bfloat16), ("aux", "orb"), scatter_dimension=2, tiled=True
    ).astype(jnp.float32)
    return (dressed.reshape(nq, 1, rows, vdev), cycle)


def line_kernel(
    dims, chol, amps_far, exps_far, table_far, dressed, cycle,
    exps, table, tiles, amps, own, rin, parts, asel, ain, wide, mine, stage, pre, pre_there, acc, cyc, csend, crecv,
    load_sem, store_sem, own_sem, fwd_sem, part_sem, in_sem, amp_sems, csend_sem, crecv_sem, amp_load_sem,
):
    nq, occ, vdev, width, groups, rows_each, norm = dims
    splits = vdev // rows_each
    pieces = nq * groups * splits
    blocks = width // occ
    me = lax.axis_index("ka")
    aux = lax.axis_index("aux")
    orb = lax.axis_index("orb")
    is_end = jnp.logical_or(me == 0, me == 3)
    is_mid = jnp.logical_not(is_end)
    near = 1 + me // 3
    outer = 3 * (me // 2)
    across = 3 - me
    peers = [(1 - aux, orb), (aux, 1 - orb), (1 - aux, 1 - orb)]

    def q_of(p):
        return p // (groups * splits)

    def group_of(p):
        return p // splits % groups

    def window(ref, p):
        high = pl.ds(pl.multiple_of(p % splits * rows_each, rows_each), rows_each)
        lanes = pl.ds(pl.multiple_of(group_of(p) * width, width), width)
        return ref.at[q_of(p), 0, high, lanes]

    def load(p):
        return pltpu.make_async_copy(window(chol, p), tiles.at[p], load_sem.at[p])

    def store(p):
        return pltpu.make_async_copy(stage.at[p], window(dressed, p), store_sem.at[p])

    def send(src, slot, p, sem, to):
        return pltpu.make_async_remote_copy(
            src_ref=src.at[p], dst_ref=rin.at[slot, p], send_sem=sem.at[p], recv_sem=in_sem.at[slot, p],
            device_id={"ka": to}, device_id_type=MESH,
        )

    def amp_send(to):
        return pltpu.make_async_remote_copy(
            src_ref=asel, dst_ref=ain, send_sem=amp_sems.at[0], recv_sem=amp_sems.at[1],
            device_id={"ka": to}, device_id_type=MESH,
        )

    def loop(n, fn):
        lax.fori_loop(0, n, lambda p, c: (fn(p), c)[1], 0)

    barrier = pltpu.get_barrier_semaphore()
    for a, o in peers:
        pl.semaphore_signal(barrier, inc=1, device_id={"aux": a, "orb": o}, device_id_type=MESH)

    @pl.when(is_end)
    def _():
        pl.semaphore_signal(barrier, inc=1, device_id={"ka": near}, device_id_type=MESH)

    @pl.when(is_mid)
    def _():
        pl.semaphore_signal(barrier, inc=1, device_id={"ka": outer}, device_id_type=MESH)
        pl.semaphore_signal(barrier, inc=1, device_id={"ka": across}, device_id_type=MESH)

    small = [
        pltpu.make_async_copy(far, here, amp_load_sem.at[n])
        for n, (far, here) in enumerate(((exps_far, exps), (table_far, table), (amps_far, amps)))
    ]
    for copy in small:
        copy.start()
    loop(pieces, lambda p: load(p).start())

    def amp(q, source):
        return amps[q, 0, table[me, source]]

    for copy in small:
        copy.wait()

    @pl.when(is_end)
    def _():
        for q in range(nq):
            for slot, source in enumerate((near, 3 - near, 3 - me)):
                asel[slot, q] = amp(q, source)

    def pack(p):
        load(p).wait()
        for n in range(width // LANES):
            here = pl.ds(n * LANES, LANES)
            shift = exps[q_of(p), 0, group_of(p) * (width // LANES) + n] + 8
            s = lax.shift_left(1, shift).astype(jnp.float32) * (1.0 / 256.0)
            own[p, :, here] = (tiles[p, :, here].astype(jnp.float32) * s).astype(jnp.bfloat16)

    def spread(ref, at, block):
        block = block.astype(jnp.float32)
        for n in range(blocks):
            strips = []
            if n > 0:
                strips.append(jnp.zeros((occ, n * occ), jnp.float32))
            strips.append(block)
            if n < blocks - 1:
                strips.append(jnp.zeros((occ, (blocks - 1 - n) * occ), jnp.float32))
            ref[(*at, pl.ds(n * occ, occ), slice(None))] = jnp.concatenate(strips, axis=1).astype(jnp.bfloat16)

    def dot(x, w):
        return lax.dot_general(x, w, (((1,), (1,)), ((), ())), preferred_element_type=jnp.float32)

    def bunch(ref, m):
        return ref[pl.ds(m * BUNCH, BUNCH)].reshape(BUNCH * rows_each, width)

    def put(ref, m, value):
        ref[pl.ds(m * BUNCH, BUNCH)] = value.reshape(BUNCH, rows_each, width)

    def finish(p, total):
        y = total.astype(jnp.bfloat16)
        stage[p] = y
        store(p).start()
        acc[q_of(p)] += lax.dot_general(y, own[p], (((0,), (0,)), ((), ())), preferred_element_type=jnp.float32)

    part = occ // 4

    def quarter(q, a, o):
        return cyc[q, pl.ds(pl.multiple_of((2 * a + o) * part, 8), part), :]

    def trade(q, n):
        a, o = peers[n]
        return pltpu.make_async_remote_copy(
            src_ref=csend.at[q, n], dst_ref=crecv.at[q, n], send_sem=csend_sem.at[q, n], recv_sem=crecv_sem.at[q, n],
            device_id={"aux": a, "orb": o}, device_id_type=MESH,
        )

    def share(q):
        cyc[q] = sum(acc[q, n * occ:(n + 1) * occ, n * occ:(n + 1) * occ] for n in range(blocks))
        for n, (a, o) in enumerate(peers):
            csend[q, n] = quarter(q, a, o)
            trade(q, n).start()

    def by_system(fn):
        each = pieces // nq
        for q in range(nq):
            lax.fori_loop(q * each, (q + 1) * each, lambda p, c: (fn(p), c)[1], 0)
            share(q)

    pl.semaphore_wait(barrier, 4 + jnp.where(is_mid, 1, 0))

    @pl.when(is_end)
    def _():
        def out(p):
            pack(p)
            send(own, 0, p, own_sem, near).start()

        out(0)
        amp_send(near).start()
        loop(pieces - 1, lambda p: out(p + 1))
        acc[...] = jnp.zeros_like(acc)
        for q in range(nq):
            spread(mine, (q,), amp(q, me))

        loop(pieces // BUNCH, lambda m: put(pre, m, dot(bunch(own, m), mine[q_of(m * BUNCH)])))

        def last(p):
            send(own, 0, p, own_sem, near).wait_recv()
            finish(p, pre[p] + rin[0, p].astype(jnp.float32))

        by_system(last)

    @pl.when(is_mid)
    def _():
        def out(p):
            send(own, 1, p, own_sem, across).start()

        loop(AHEAD, lambda p: (pack(p), out(p)))
        loop(pieces - AHEAD, lambda p: pack(p + AHEAD))
        acc[...] = jnp.zeros_like(acc)
        for q in range(nq):
            spread(mine, (q,), amp(q, outer))
            for slot, source in enumerate((me, across, 3 - outer)):
                spread(wide, (slot, q, 0), amp(q, source))
        amp_send(outer).wait_recv()
        for q in range(nq):
            for slot in range(3):
                spread(wide, (slot, q, 1), ain[slot, q])

        def early(m):
            for n in range(BUNCH):
                p = m * BUNCH + n
                send(own, 0, p, own_sem, outer).wait_recv()
                send(rin.at[0], 2, p, fwd_sem, across).start()

                @pl.when(p + AHEAD < pieces)
                def _():
                    out(p + AHEAD)

            q = q_of(m * BUNCH)
            x = bunch(own, m)
            there = dot(x, wide[0, q, 1])
            here = dot(x, wide[0, q, 0]) + dot(bunch(rin.at[0], m), mine[q])
            for n in range(BUNCH):
                send(own, 1, m * BUNCH + n, own_sem, across).wait_recv()
            x = bunch(rin.at[1], m)
            put(pre_there, m, there + dot(x, wide[1, q, 1]))
            put(pre, m, here + dot(x, wide[1, q, 0]))

        def last(p):
            q = q_of(p)
            send(own, 2, p, own_sem, across).wait_recv()
            parts[p] = (pre_there[p] + dot(rin[2, p], wide[2, q, 1])).astype(jnp.bfloat16)
            send(parts, 0, p, part_sem, outer).start()
            finish(p, pre[p] + dot(rin[2, p], wide[2, q, 0]))

        def turn(p):
            @pl.when(p < pieces)
            def _():
                early(p)

            @pl.when(p >= LAG)
            def _():
                last(p - LAG)

            for q in range(nq):
                @pl.when(p == LAG + (q + 1) * (pieces // nq) - 1)
                def _():
                    share(q)

        loop(pieces + LAG, turn)

    for q in range(nq):
        total = quarter(q, aux, orb)
        for n in range(3):
            trade(q, n).wait_recv()
            total += crecv[q, n]
        cycle[q, 0] = total * norm

    for q in range(nq):
        for n in range(3):
            trade(q, n).wait_send()
    loop(pieces, lambda p: store(p).wait())
    loop(pieces, lambda p: send(own, 0, p, own_sem, near).wait_send())

    @pl.when(is_end)
    def _():
        amp_send(near).wait_send()

    @pl.when(is_mid)
    def _():
        loop(pieces, lambda p: send(own, 2, p, fwd_sem, across).wait_send())
        loop(pieces, lambda p: send(own, 0, p, part_sem, outer).wait_send())


def line_body(chol_tiles, tile_exps, amplitudes, pair_table):
    nq, _, rows, vdev = chol_tiles.shape
    occ = amplitudes.shape[-1]
    width = math.lcm(occ, LANES)
    groups = rows // width
    pieces = nq * groups * (vdev // ROWS_EACH)
    devices = lax.axis_size("aux") * lax.axis_size("orb")
    norm = (rows // occ * vdev * devices) ** -0.5
    bf16, f32 = jnp.bfloat16, jnp.float32
    dma = pltpu.SemaphoreType.DMA
    part = occ // devices
    turned = jnp.swapaxes(chol_tiles, 2, 3)
    dressed, cycle = pl.pallas_call(
        functools.partial(line_kernel, (nq, occ, vdev, width, groups, ROWS_EACH, norm)),
        out_shape=(
            jax.ShapeDtypeStruct(turned.shape, bf16),
            jax.ShapeDtypeStruct((nq, 1, part, occ), f32),
        ),
        in_specs=[
            pl.BlockSpec(memory_space=pltpu.HBM),
            pl.BlockSpec(memory_space=pltpu.HBM),
            pl.BlockSpec(memory_space=pltpu.HBM),
            pl.BlockSpec(memory_space=pltpu.HBM),
        ],
        out_specs=(pl.BlockSpec(memory_space=pltpu.HBM), pl.BlockSpec(memory_space=pltpu.VMEM)),
        scratch_shapes=[
            pltpu.SMEM(tile_exps.shape, jnp.int32),
            pltpu.SMEM(pair_table.shape, jnp.int32),
            pltpu.VMEM((pieces, ROWS_EACH, width), bf16),
            pltpu.VMEM(amplitudes.shape, bf16),
            pltpu.VMEM((pieces, ROWS_EACH, width), bf16),
            pltpu.VMEM((3, pieces, ROWS_EACH, width), bf16),
            pltpu.VMEM((pieces, ROWS_EACH, width), bf16),
            pltpu.VMEM((3, nq, occ, occ), bf16),
            pltpu.VMEM((3, nq, occ, occ), bf16),
            pltpu.VMEM((3, nq, 2, width, width), bf16),
            pltpu.VMEM((nq, width, width), bf16),
            pltpu.VMEM((pieces, ROWS_EACH, width), bf16),
            pltpu.VMEM((pieces, ROWS_EACH, width), f32),
            pltpu.VMEM((pieces, ROWS_EACH, width), f32),
            pltpu.VMEM((nq, width, width), f32),
            pltpu.VMEM((nq, occ, occ), f32),
            pltpu.VMEM((nq, 3, part, occ), f32),
            pltpu.VMEM((nq, 3, part, occ), f32),
            dma((pieces,)),
            dma((pieces,)),
            dma((pieces,)),
            dma((pieces,)),
            dma((pieces,)),
            dma((3, pieces)),
            dma((2,)),
            dma((nq, 3)),
            dma((nq, 3)),
            dma((3,)),
        ],
        compiler_params=pltpu.CompilerParams(
            collective_id=0, has_side_effects=True, vmem_limit_bytes=60 * 1024 * 1024
        ),
        cost_estimate=pl.CostEstimate(
            flops=2 * 8 * occ * rows * vdev * nq, bytes_accessed=4 * rows * nq * vdev, transcendentals=0
        ),
    )(turned, amplitudes, tile_exps, pair_table)

    def hand_on(near_out, near_cycle, far_out, far_cycle, held, held_cycle, sems):
        parts = [(q, 0, pl.ds(n * vdev // 2, vdev // 2)) for q in range(nq) for n in range(2)]
        trips = [(near_cycle, held_cycle, far_cycle)] + [(near_out.at[i], held.at[i], far_out.at[i]) for i in parts]
        ins = [pltpu.make_async_copy(a, b, sems.at[0, n]) for n, (a, b, _) in enumerate(trips)]
        outs = [pltpu.make_async_copy(b, c, sems.at[1, n]) for n, (_, b, c) in enumerate(trips)]
        for copy in ins:
            copy.start()
        for before, after in zip(ins, outs):
            before.wait()
            after.start()
        for copy in outs:
            copy.wait()

    dressed, cycle = pl.pallas_call(
        hand_on,
        out_shape=(
            jax.ShapeDtypeStruct(dressed.shape, dressed.dtype),
            jax.ShapeDtypeStruct(cycle.shape, cycle.dtype),
        ),
        in_specs=[pl.BlockSpec(memory_space=pltpu.HBM)] * 2,
        out_specs=(pl.BlockSpec(memory_space=pltpu.HBM),) * 2,
        scratch_shapes=[
            pltpu.VMEM(dressed.shape, dressed.dtype),
            pltpu.VMEM(cycle.shape, cycle.dtype),
            dma((2, 1 + 2 * nq)),
        ],
        compiler_params=pltpu.CompilerParams(vmem_limit_bytes=60 * 1024 * 1024),
        name="hand_on",
    )(dressed, cycle)
    return jnp.swapaxes(dressed, 2, 3), cycle


def solution(mesh):
    def body(chol_tiles, tile_exps, amplitudes, pair_table):
        nq, _, rows, vdev = chol_tiles.shape
        occ = amplitudes.shape[-1]
        line = mesh.shape["ka"] == 4 and mesh.shape["aux"] == 2 and mesh.shape["orb"] == 2
        fits = rows % math.lcm(occ, LANES) == 0 and vdev % (BUNCH * ROWS_EACH) == 0 and occ % 32 == 0
        fits = fits and nq * rows * vdev >= AHEAD * math.lcm(occ, LANES) * ROWS_EACH
        chosen = line_body if line and fits else ring_body
        return chosen(chol_tiles, tile_exps, amplitudes, pair_table)

    return jax.shard_map(
        body,
        mesh=mesh,
        in_specs=(
            P("grp", "ka", "aux", "orb"),
            P("grp", "ka", "aux"),
            P("grp", "ka", None, None, None),
            P(),
        ),
        out_specs=(P("grp", "ka", "aux", "orb"), P("grp", "ka", ("aux", "orb"), None)),
        check_vma=False,
    )
```
